32 devices in a mesh: group: 8 (over z, y), inner: 4 (over x, core).
Axes of the slice: x: 2, y: 2, z: 4, core: 2. Of those that a mesh axis runs over, the one named last changes fastest.
Arguments:
- tokens: bfloat16 [12288, 4096], P(('group', 'inner')), may hold values from -6 to 6
- master_weight: float32 [4096, 768], P('inner', 'group'), may hold values from -0.09375 to 0.09375
- first_moment: float32 [4096, 768], P('inner', 'group'), may hold values from -6 to 6
- second_moment: float32 [4096, 768], P('inner', 'group'), may hold values from 0.1 to 10
- gradient: float32 [4096, 768], P('inner', 'group'), may hold values from -6 to 6
- gate_weight: bfloat16 [4096, 2], P('inner'), may hold values from -0.09375 to 0.09375
- input_bias: float32 [1], replicated, may hold values from -3 to -1
- forget_bias: float32 [1], replicated, may hold values from 2 to 5
Outputs:
- new_master: float32 [4096, 768], P('inner', 'group')
- new_first: float32 [4096, 768], P('inner', 'group')
- new_second: float32 [4096, 768], P('inner', 'group')
- hidden: bfloat16 [12288, 256], P(('group', 'inner'))
The draws below stay inside these ranges and needn't reach their ends.
All inputs are finite; a program needn't handle non-finite values.
Results may differ from the reference program's by a relative error of at most 0.012.
Values may be sent and summed in bfloat16 or wider, within the bound.
No kernel may reach another device: no remote copies, remote signals or barrier semaphores. Data moves between devices by JAX's collectives and lax.ppermute only.
A program may use at most 64 MiB of HBM per device.

```python
import math
import jax
import jax.numpy as jnp
from jax import lax

D = 4096
QK = 256
V = 256
TOK_DEV = 384
PROJ = 768
TOKENS = 12288


def levels(key, extent, shards, low, top_value):
    gain, own = 1.0, jax.random.fold_in(key, 6)
    for dim, blocks in shards:
        draws = jnp.exp(jax.random.uniform(jax.random.fold_in(own, dim), (blocks,), jnp.float32, low / len(shards), top_value / len(shards)))
        gain = gain * jnp.repeat(draws, extent[dim] // blocks).reshape([-1 if axis == dim else 1 for axis in range(len(extent))])
    return gain


def normal_values(key, dims, deviation, limit, split=(), dtype=jnp.bfloat16):
    values = deviation * jax.random.normal(key, dims, jnp.float32)
    if split:
        values = values * levels(key, dims, split, -0.22, 0.18)
    return jnp.clip(values, -limit, limit).astype(dtype)


def setup_inputs(seed: int = 0) -> dict:
    seeds = jax.random.split(jax.random.key(seed), 9)
    return {
        "tokens": normal_values(seeds[0], (TOKENS, D), 1.0, 6.0, ((0, 32),)),
        "master_weight": normal_values(seeds[1], (D, PROJ), D ** -0.5, 0.09375, ((0, 4), (1, 8)), jnp.float32),
        "first_moment": normal_values(seeds[2], (D, PROJ), 1.0, 6.0, ((0, 4), (1, 8)), jnp.float32),
        "second_moment": jnp.clip(jnp.exp(math.log(10.0) - 4.6051702 * jax.random.uniform(seeds[3], (D, PROJ), jnp.float32) ** levels(seeds[3], (D, PROJ), ((0, 4), (1, 8)), -0.2, 0.2)), 0.1, 10.0),
        "gradient": normal_values(seeds[4], (D, PROJ), 1.0, 6.0, ((0, 4), (1, 8)), jnp.float32),
        "gate_weight": normal_values(seeds[5], (D, 2), D ** -0.5, 0.09375, ((0, 4),)),
        "input_bias": jnp.clip(jax.random.uniform(seeds[6], (1,), jnp.float32, -3.0, -1.0), -3.0, -1.0),
        "forget_bias": jnp.clip(jax.random.uniform(seeds[7], (1,), jnp.float32, 2.0, 5.0), 2.0, 5.0),
    }


beta_first = 0.9
beta_second = 0.999
learn_rate = 0.001
adam_eps = 1e-08
fix_first = 1.0 - (0.9 ** 10) ** 10
fix_second = 1.0 - (0.999 ** 10) ** 10

def mlstm_head(sequence, projected, gate_pre, input_bias, forget_bias):
    query_rows = projected[:, :QK].astype(jnp.bfloat16)
    key_rows = projected[:, QK:2 * QK].astype(jnp.bfloat16)
    value_rows = projected[:, 2 * QK:].astype(jnp.bfloat16)
    input_gate = gate_pre[:, 0] + input_bias[0]
    forget_log = jax.nn.log_sigmoid(gate_pre[:, 1] + forget_bias[0])
    cumulative = jnp.cumsum(forget_log)
    row_count = sequence.shape[0]
    causal = jnp.arange(row_count)[:, None] >= jnp.arange(row_count)[None, :]
    decay_log = cumulative[:, None] - cumulative[None, :] + input_gate[None, :]
    decay_matrix = jnp.exp(jnp.where(causal, decay_log, -jnp.inf))
    scores = jnp.dot(query_rows, key_rows.T, preferred_element_type=jnp.float32) * QK ** (-0.5)
    weighted = scores * decay_matrix
    normalizer = lax.optimization_barrier(jnp.sum(weighted, axis=1))
    numerator = jnp.dot(weighted.astype(jnp.bfloat16), value_rows, preferred_element_type=jnp.float32)
    return (numerator / jnp.maximum(jnp.abs(normalizer), 1.0)[:, None]).astype(jnp.bfloat16)

def reference(tokens, master_weight, first_moment, second_moment, gradient, gate_weight, input_bias, forget_bias):
    new_first = beta_first * first_moment + (1.0 - beta_first) * gradient
    new_second = beta_second * second_moment + (1.0 - beta_second) * gradient * gradient
    new_master = master_weight - learn_rate * (new_first / fix_first) / (jnp.sqrt(new_second / fix_second) + adam_eps)
    weights = new_master.astype(jnp.bfloat16)

    def mix_sequence(sequence):
        projected = jnp.dot(sequence, weights, preferred_element_type=jnp.float32)
        gate_pre = jnp.dot(sequence, gate_weight, preferred_element_type=jnp.float32)
        return mlstm_head(sequence, projected, gate_pre, input_bias, forget_bias)
    hidden = lax.map(mix_sequence, tokens.reshape(-1, TOK_DEV, D))
    return (new_master, new_first, new_second, hidden.reshape(-1, V))
```

```python
import functools
import itertools

import jax
import jax.numpy as jnp
from jax import lax
from jax.experimental import pallas as pl
from jax.experimental.pallas import tpu as pltpu
from jax.sharding import PartitionSpec as P

QK = 256


beta_first = 0.9
beta_second = 0.999
learn_rate = 0.001
adam_eps = 1e-08
fix_first = 1.0 - (0.9**10) ** 10
fix_second = 1.0 - (0.999**10) ** 10

AXES = ("group", "inner")
NT = (((1,), (1,)), ((), ()))
TN = (((0,), (0,)), ((), ()))


def adam(first_moment, second_moment, master_weight, gradient):
    new_first = beta_first * first_moment + (1.0 - beta_first) * gradient
    new_second = beta_second * second_moment + (1.0 - beta_second) * gradient * gradient
    new_master = master_weight - learn_rate * (new_first / fix_first) / (
        jnp.sqrt(new_second / fix_second) + adam_eps
    )
    return new_master, new_first, new_second


def mlstm_head(sequence, projected, gate_pre, input_bias, forget_bias):
    query_rows = projected[:, :QK].astype(jnp.bfloat16)
    key_rows = projected[:, QK : 2 * QK].astype(jnp.bfloat16)
    value_rows = projected[:, 2 * QK :].astype(jnp.bfloat16)
    input_gate = gate_pre[:, 0] + input_bias[0]
    forget_log = jax.nn.log_sigmoid(gate_pre[:, 1] + forget_bias[0])
    cumulative = jnp.cumsum(forget_log)
    row_count = sequence.shape[0]
    causal = jnp.arange(row_count)[:, None] >= jnp.arange(row_count)[None, :]
    decay_log = cumulative[:, None] - cumulative[None, :] + input_gate[None, :]
    decay_matrix = jnp.exp(jnp.where(causal, decay_log, -jnp.inf))
    scores = jnp.dot(query_rows, key_rows.T, preferred_element_type=jnp.float32) * QK ** (-0.5)
    weighted = scores * decay_matrix
    normalizer = jnp.sum(weighted, axis=1)
    numerator = jnp.dot(
        weighted.astype(jnp.bfloat16), value_rows, preferred_element_type=jnp.float32
    )
    return (numerator / jnp.maximum(jnp.abs(normalizer), 1.0)[:, None]).astype(jnp.bfloat16)


def gathered_everywhere(
    tokens, master_weight, first_moment, second_moment, gradient, gate_weight, input_bias, forget_bias
):
    new_master, new_first, new_second = adam(first_moment, second_moment, master_weight, gradient)
    sendable = new_master.astype(jnp.bfloat16)
    secondary = lax.all_gather(sendable, "group", axis=1, tiled=True)
    projected = jnp.dot(
        tokens,
        lax.all_gather(secondary, "inner", axis=0, tiled=True),
        preferred_element_type=jnp.float32,
    )
    gate_pre = jnp.dot(
        tokens,
        lax.all_gather(gate_weight, "inner", axis=0, tiled=True),
        preferred_element_type=jnp.float32,
    )
    hidden = mlstm_head(tokens, projected, gate_pre, input_bias, forget_bias)
    return (new_master, new_first, new_second, hidden)


NZ, NY, NX, NC = 4, 2, 2, 2


def permutation(target):
    pairs = []
    for z, y, x, c in itertools.product(range(NZ), range(NY), range(NX), range(NC)):
        to_z, to_y, to_x, to_c = target(z, y, x, c)
        pairs.append((((z * NY + y) * NX + x) * NC + c, ((to_z * NY + to_y) * NX + to_x) * NC + to_c))
    return pairs


OTHER_CORE = permutation(lambda z, y, x, c: (z, y, x, 1 - c))
OTHER_X = permutation(lambda z, y, x, c: (z, y, 1 - x, c))
NEXT_Z = permutation(lambda z, y, x, c: ((z + 1) % NZ, y, x, c))
FIRST = permutation(lambda z, y, x, c: (z, y, 1 - x, c) if c == 0 else (z, 1 - y, x, c))
SECOND = permutation(lambda z, y, x, c: (z, 1 - y, x, c) if c == 0 else (z, y, 1 - x, c))


def send(block, pairs):
    return lax.ppermute(block, AXES, pairs)


def place():
    group, inner = lax.axis_index("group"), lax.axis_index("inner")
    return group // NY, group % NY, inner // NC, inner % NC


def adam_kernel(master_ref, first_ref, second_ref, grad_ref, to_master, to_first, to_second, to_send):
    new_master, new_first, new_second = adam(
        first_ref[...], second_ref[...], master_ref[...], grad_ref[...]
    )
    to_master[...] = new_master
    to_first[...] = new_first
    to_second[...] = new_second
    to_send[...] = new_master.astype(jnp.bfloat16)


def adam_step(master, first, second, grad):
    columns, rows = master.shape
    steps = 3
    spec = pl.BlockSpec((columns // steps, rows), lambda i: (i, 0))
    wide = jax.ShapeDtypeStruct(master.shape, jnp.float32)
    return pl.pallas_call(
        adam_kernel,
        grid=(steps,),
        in_specs=[spec] * 4,
        out_specs=[spec] * 4,
        out_shape=[wide, wide, wide, jax.ShapeDtypeStruct(master.shape, jnp.bfloat16)],
        name="adam",
    )(master, first, second, grad)


def project_kernel(with_gate, own_block, first_block, second_block, third_block, *rest):
    if with_gate:
        own_gate, other_gate, tokens, tokens_other, out_own, out_send, stack, held, piece_sem, token_sem = rest
    else:
        tokens, tokens_other, out_own, out_send, stack, held, piece_sem, token_sem = rest
    _, y, x, c = place()
    columns, depth = own_block.shape
    here = pl.multiple_of(y * columns, 16)
    there = pl.multiple_of((1 - y) * columns, 16)
    swap = c == 0
    spots = [
        (own_block, 0, here),
        (first_block, jnp.where(swap, 1, 0), jnp.where(swap, here, there)),
        (second_block, jnp.where(swap, 0, 1), jnp.where(swap, there, here)),
        (third_block, 1, there),
    ]
    copies = []
    for side, its_x in enumerate((x, 1 - x)):
        at = pl.multiple_of((its_x * NC + c) * depth, depth)
        for which, source in enumerate((tokens, tokens_other)):
            copies.append(
                pltpu.make_async_copy(
                    source.at[:, pl.ds(at, depth)], held.at[side, which], token_sem.at[side, which]
                )
            )
    pieces = [
        pltpu.make_async_copy(
            source, stack.at[side, pl.ds(pl.multiple_of(row, 16), columns)], piece_sem.at[n]
        )
        for n, (source, side, row) in enumerate(spots)
    ]
    for copy in pieces + copies:
        copy.start()
    if with_gate:
        for side, gate in enumerate((own_gate, other_gate)):
            stack[side, NY * columns :] = jnp.concatenate(
                [gate[...], jnp.zeros((16 - gate.shape[0], depth), jnp.bfloat16)], axis=0
            )
    for copy in pieces:
        copy.wait()
    sums = [None, None]
    for side in range(2):
        for which in range(2):
            copies[side * 2 + which].wait()
            part = lax.dot_general(
                stack[side], held[side, which], NT, preferred_element_type=jnp.float32
            )
            sums[which] = part if side == 0 else sums[which] + part
    out_own[...] = sums[0]
    out_send[...] = sums[1]


def project(blocks, gates, tokens, tokens_other):
    columns, depth = blocks[0].shape
    rows = NY * columns + (16 if gates else 0)
    sequence = tokens.shape[0]
    any_spec = pl.BlockSpec(memory_space=pl.ANY)
    vmem_spec = pl.BlockSpec(memory_space=pltpu.VMEM)
    out = jax.ShapeDtypeStruct((rows, sequence), jnp.float32)
    return pl.pallas_call(
        functools.partial(project_kernel, bool(gates)),
        in_specs=[any_spec] * 4 + [vmem_spec] * len(gates) + [any_spec] * 2,
        out_specs=[vmem_spec] * 2,
        out_shape=[out, out],
        scratch_shapes=[
            pltpu.VMEM((2, rows, depth), jnp.bfloat16),
            pltpu.VMEM((2, 2, sequence, depth), jnp.bfloat16),
            pltpu.SemaphoreType.DMA((4,)),
            pltpu.SemaphoreType.DMA((2, 2)),
        ],
        compiler_params=pltpu.CompilerParams(vmem_limit_bytes=20 * 2**20),
        cost_estimate=pl.CostEstimate(
            flops=2 * 2 * 2 * rows * depth * sequence, bytes_accessed=2 * 4 * sequence * depth, transcendentals=0
        ),
        name="project",
    )(*blocks, *gates, tokens, tokens_other)


def head_kernel(own_0, own_1, own_2, own_3, got_0, got_1, got_2, got_3, input_bias, forget_bias, out, projected):
    z, _, _, _ = place()
    columns = own_1.shape[0]
    sequence = own_1.shape[1]
    for offset, (own, got) in enumerate(((own_0, got_0), (own_1, got_1), (own_2, got_2), (own_3, got_3))):
        at = pl.multiple_of(lax.rem(z + NZ - offset, NZ) * columns, 16)
        projected[pl.ds(at, columns)] = (own[:columns] + got[:columns]).astype(jnp.bfloat16)
    gate_pre = own_0[columns : columns + 8] + got_0[columns : columns + 8]
    input_gate = gate_pre[0:1] + input_bias[0]
    cumulative = jax.nn.log_sigmoid(gate_pre[1:2] + forget_bias[0])
    lane = lax.broadcasted_iota(jnp.int32, (1, sequence), 1)
    step = 1
    while step < sequence:
        cumulative = cumulative + jnp.where(lane >= step, pltpu.roll(cumulative, step, 1), 0.0)
        step *= 2
    source = jnp.broadcast_to(input_gate - cumulative, (8, sequence)).T[:, 0:1]
    to_t = lax.broadcasted_iota(jnp.int32, (sequence, sequence), 1)
    from_s = lax.broadcasted_iota(jnp.int32, (sequence, sequence), 0)
    decay = jnp.exp(jnp.where(from_s <= to_t, cumulative + source, -jnp.inf))
    query, key, value = (projected[n * QK : (n + 1) * QK] for n in range(3))
    scores = lax.dot_general(key, query, TN, preferred_element_type=jnp.float32) * QK ** (-0.5)
    weighted = scores * decay
    normalizer = jnp.sum(weighted, axis=0, keepdims=True)
    numerator = jnp.dot(value, weighted.astype(jnp.bfloat16), preferred_element_type=jnp.float32)
    out[...] = (numerator / jnp.maximum(jnp.abs(normalizer), 1.0)).T.astype(jnp.bfloat16)


def head(own, got, input_bias, forget_bias):
    columns, sequence = own[1].shape
    vmem_spec = pl.BlockSpec(memory_space=pltpu.VMEM)
    smem_spec = pl.BlockSpec(memory_space=pltpu.SMEM)
    return pl.pallas_call(
        head_kernel,
        in_specs=[vmem_spec] * 8 + [smem_spec] * 2,
        out_specs=vmem_spec,
        out_shape=jax.ShapeDtypeStruct((sequence, NZ * columns - 2 * QK), jnp.bfloat16),
        scratch_shapes=[pltpu.VMEM((NZ * columns, sequence), jnp.bfloat16)],
        compiler_params=pltpu.CompilerParams(vmem_limit_bytes=20 * 2**20),
        name="head",
    )(*own, *got, input_bias, forget_bias)


def after(value, *others):
    return lax.optimization_barrier((value,) + others)[0]


def by_links(
    tokens, master_weight, first_moment, second_moment, gradient, gate_weight, input_bias, forget_bias
):
    new_master, new_first, new_second, block = adam_step(
        master_weight.T, first_moment.T, second_moment.T, gradient.T
    )
    gate = gate_weight.T
    z1 = send(block, NEXT_Z)
    a1 = send(block, FIRST)
    a2 = send(block, SECOND)
    tokens_other = send(tokens, OTHER_CORE)
    gate_other = send(gate, OTHER_X)
    go = after(z1, a1, a2)
    b1 = send(go, FIRST)
    a3 = send(a1, SECOND)
    z2 = send(go, NEXT_Z)
    b2 = send(go, SECOND)
    own_a, part_a = project((block, a1, a2, a3), (gate, gate_other), tokens, tokens_other)
    go = after(z2, b1, a3)
    c1 = send(go, FIRST)
    b3 = send(b1, SECOND)
    z3 = send(go, NEXT_Z)
    c2 = send(go, SECOND)
    own_b, part_b = project((z1, b1, b2, b3), (), tokens, tokens_other)
    go = after(z3, c1, b3)
    d1 = send(go, FIRST)
    c3 = send(c1, SECOND)
    d2 = send(go, SECOND)
    own_c, part_c = project((z2, c1, c2, c3), (), tokens, tokens_other)
    d3 = send(d1, SECOND)
    own_d, part_d = project((z3, d1, d2, d3), (), tokens, tokens_other)
    got = [send(part, OTHER_CORE) for part in (part_a, part_b, part_c, part_d)]
    hidden = head((own_a, own_b, own_c, own_d), got, input_bias, forget_bias)
    return (new_master.T, new_first.T, new_second.T, hidden)


def solution(mesh):
    placed = (
        P(("group", "inner"), None),
        P("inner", "group"),
        P("inner", "group"),
        P("inner", "group"),
        P("inner", "group"),
        P("inner", None),
        P(),
        P(),
    )
    fits = mesh.shape["group"] == NZ * NY and mesh.shape["inner"] == NX * NC
    return jax.shard_map(
        by_links if fits else gathered_everywhere,
        mesh=mesh,
        in_specs=placed,
        out_specs=(
            P("inner", "group"),
            P("inner", "group"),
            P("inner", "group"),
            P(("group", "inner"), None),
        ),
        check_vma=False,
    )
```

```python
import functools
import itertools

import jax
import jax.numpy as jnp
from jax import lax
from jax.experimental import pallas as pl
from jax.experimental.pallas import tpu as pltpu
from jax.sharding import PartitionSpec as P

QK = 256


beta_first = 0.9
beta_second = 0.999
learn_rate = 0.001
adam_eps = 1e-08
fix_first = 1.0 - (0.9**10) ** 10
fix_second = 1.0 - (0.999**10) ** 10

AXES = ("group", "inner")
NT = (((1,), (1,)), ((), ()))
TN = (((0,), (0,)), ((), ()))


def adam(first_moment, second_moment, master_weight, gradient):
    new_first = beta_first * first_moment + (1.0 - beta_first) * gradient
    new_second = beta_second * second_moment + (1.0 - beta_second) * gradient * gradient
    new_master = master_weight - learn_rate * (new_first / fix_first) / (
        jnp.sqrt(new_second / fix_second) + adam_eps
    )
    return new_master, new_first, new_second


def mlstm_head(sequence, projected, gate_pre, input_bias, forget_bias):
    query_rows = projected[:, :QK].astype(jnp.bfloat16)
    key_rows = projected[:, QK : 2 * QK].astype(jnp.bfloat16)
    value_rows = projected[:, 2 * QK :].astype(jnp.bfloat16)
    input_gate = gate_pre[:, 0] + input_bias[0]
    forget_log = jax.nn.log_sigmoid(gate_pre[:, 1] + forget_bias[0])
    cumulative = jnp.cumsum(forget_log)
    row_count = sequence.shape[0]
    causal = jnp.arange(row_count)[:, None] >= jnp.arange(row_count)[None, :]
    decay_log = cumulative[:, None] - cumulative[None, :] + input_gate[None, :]
    decay_matrix = jnp.exp(jnp.where(causal, decay_log, -jnp.inf))
    scores = jnp.dot(query_rows, key_rows.T, preferred_element_type=jnp.float32) * QK ** (-0.5)
    weighted = scores * decay_matrix
    normalizer = jnp.sum(weighted, axis=1)
    numerator = jnp.dot(
        weighted.astype(jnp.bfloat16), value_rows, preferred_element_type=jnp.float32
    )
    return (numerator / jnp.maximum(jnp.abs(normalizer), 1.0)[:, None]).astype(jnp.bfloat16)


def gathered_everywhere(
    tokens, master_weight, first_moment, second_moment, gradient, gate_weight, input_bias, forget_bias
):
    new_master, new_first, new_second = adam(first_moment, second_moment, master_weight, gradient)
    sendable = new_master.astype(jnp.bfloat16)
    secondary = lax.all_gather(sendable, "group", axis=1, tiled=True)
    projected = jnp.dot(
        tokens,
        lax.all_gather(secondary, "inner", axis=0, tiled=True),
        preferred_element_type=jnp.float32,
    )
    gate_pre = jnp.dot(
        tokens,
        lax.all_gather(gate_weight, "inner", axis=0, tiled=True),
        preferred_element_type=jnp.float32,
    )
    hidden = mlstm_head(tokens, projected, gate_pre, input_bias, forget_bias)
    return (new_master, new_first, new_second, hidden)


NZ, NY, NX, NC = 4, 2, 2, 2


def permutation(target):
    pairs = []
    for z, y, x, c in itertools.product(range(NZ), range(NY), range(NX), range(NC)):
        to_z, to_y, to_x, to_c = target(z, y, x, c)
        pairs.append((((z * NY + y) * NX + x) * NC + c, ((to_z * NY + to_y) * NX + to_x) * NC + to_c))
    return pairs


OTHER_CORE = permutation(lambda z, y, x, c: (z, y, x, 1 - c))
OTHER_X = permutation(lambda z, y, x, c: (z, y, 1 - x, c))
FLIP_Z = [permutation(lambda z, y, x, c, flip=flip: (z ^ flip, y, x, c)) for flip in range(NZ)]
FIRST = permutation(lambda z, y, x, c: (z, y, 1 - x, c) if c == 0 else (z, 1 - y, x, c))
SECOND = permutation(lambda z, y, x, c: (z, 1 - y, x, c) if c == 0 else (z, y, 1 - x, c))


def send(block, pairs):
    return lax.ppermute(block, AXES, pairs)


def place():
    group, inner = lax.axis_index("group"), lax.axis_index("inner")
    return group // NY, group % NY, inner // NC, inner % NC


GATE_ROWS = 16


def adam_kernel(
    master_ref, first_ref, second_ref, grad_ref, gate_ref, to_master, to_first, to_second, to_send, to_send_gated
):
    new_master, new_first, new_second = adam(
        first_ref[...], second_ref[...], master_ref[...], grad_ref[...]
    )
    to_master[...] = new_master
    to_first[...] = new_first
    to_second[...] = new_second
    rows = new_master.shape[0]
    at = pl.ds(pl.multiple_of(pl.program_id(0) * rows, 16), rows)
    to_send[at] = new_master.astype(jnp.bfloat16)
    to_send_gated[at] = new_master.astype(jnp.bfloat16)

    @pl.when(pl.program_id(0) == 0)
    def _():
        gate = gate_ref[...]
        pad = jnp.zeros((GATE_ROWS - gate.shape[0], gate.shape[1]), gate.dtype)
        to_send_gated[to_send.shape[0] :] = jnp.concatenate([gate, pad], axis=0)


def adam_step(master, first, second, grad, gate):
    columns, rows = master.shape
    steps = 2
    spec = pl.BlockSpec((columns // steps, rows), lambda i: (i, 0))
    wide = jax.ShapeDtypeStruct(master.shape, jnp.float32)
    sent = [(columns, rows), (columns + GATE_ROWS, rows)]
    return pl.pallas_call(
        adam_kernel,
        grid=(steps,),
        in_specs=[spec] * 4 + [pl.BlockSpec(gate.shape, lambda i: (0, 0))],
        out_specs=[spec] * 3 + [pl.BlockSpec(shape, lambda i: (0, 0)) for shape in sent],
        out_shape=[wide] * 3 + [jax.ShapeDtypeStruct(shape, jnp.bfloat16) for shape in sent],
        name="adam",
    )(master, first, second, grad, gate)


VMEM = pl.BlockSpec(memory_space=pltpu.VMEM)
SMEM = pl.BlockSpec(memory_space=pltpu.SMEM)
HBM = pl.BlockSpec(memory_space=pltpu.HBM)
ROOM = pltpu.CompilerParams(vmem_limit_bytes=20 * 2**20)

def hold_kernel(tokens, gated, held, held_gated, sems):
    copies = [
        pltpu.make_async_copy(source, target, sems.at[n])
        for n, (source, target) in enumerate(((tokens, held), (gated, held_gated)))
    ]
    for copy in copies:
        copy.start()
    for copy in copies:
        copy.wait()


def hold(tokens, gated):
    return pl.pallas_call(
        hold_kernel,
        in_specs=[HBM] * 2,
        out_specs=[VMEM] * 2,
        out_shape=[jax.ShapeDtypeStruct(array.shape, array.dtype) for array in (tokens, gated)],
        scratch_shapes=[pltpu.SemaphoreType.DMA((2,))],
        compiler_params=ROOM,
        cost_estimate=pl.CostEstimate(flops=0, bytes_accessed=31457280, transcendentals=0),
        name="hold",
    )(tokens, gated)


def row_block(its_x, its_c, depth):
    return pl.ds(pl.multiple_of((its_x * NC + its_c) * depth, depth), depth)


def project_kernel(columns, gated, *refs):
    blocks, (tokens, tokens_other, out_own, out_send, stack) = refs[:-5], refs[-5:]
    _, y, x, c = place()
    depth = blocks[0].shape[1]
    swap = c == 0
    spots = (
        (0, y),
        (jnp.where(swap, 1, 0), jnp.where(swap, y, 1 - y)),
        (jnp.where(swap, 0, 1), jnp.where(swap, 1 - y, y)),
        (1, 1 - y),
    )
    for block, (side, its_y) in zip(blocks, spots):
        stack[side, pl.ds(pl.multiple_of(its_y * columns, 16), columns)] = block[:columns]
    if len(blocks) == 3:
        side, its_y = spots[3]
        stack[side, pl.ds(pl.multiple_of(its_y * columns, 16), columns)] = jnp.zeros(
            (columns, depth), jnp.bfloat16
        )
    if gated:
        _, first, second = (block[columns:] for block in blocks[:3])
        stack[0, NY * columns :] = blocks[0][columns:]
        stack[1, NY * columns :] = jnp.where(swap, first, second)
    for source, out in ((tokens_other, out_send), (tokens, out_own)):
        parts = [
            lax.dot_general(
                stack[side], source[:, row_block(its_x, c, depth)], NT, preferred_element_type=jnp.float32
            )
            for side, its_x in enumerate((x, 1 - x))
        ]
        out[...] = parts[0] + parts[1]


def project(columns, blocks, tokens, tokens_other):
    its_rows, depth = blocks[0].shape
    gated = its_rows > columns
    rows = NY * columns + (GATE_ROWS if gated else 0)
    sequence = tokens.shape[0]
    out = jax.ShapeDtypeStruct((rows, sequence), jnp.float32)
    return pl.pallas_call(
        functools.partial(project_kernel, columns, gated),
        in_specs=[VMEM] * (len(blocks) + 2),
        out_specs=[VMEM] * 2,
        out_shape=[out, out],
        scratch_shapes=[pltpu.VMEM((NX, rows, depth), jnp.bfloat16)],
        compiler_params=ROOM,
        cost_estimate=pl.CostEstimate(
            flops=2 * 2 * NX * rows * depth * sequence, bytes_accessed=8 * sequence * depth, transcendentals=0
        ),
        name="project",
    )(*blocks, tokens, tokens_other)


def decay_kernel(own, got, input_bias, forget_bias, out):
    rows, sequence = own.shape
    gate_pre = own[rows - GATE_ROWS : rows - 8] + got[rows - GATE_ROWS : rows - 8]
    input_gate = gate_pre[0:1] + input_bias[0]
    cumulative = jax.nn.log_sigmoid(gate_pre[1:2] + forget_bias[0])
    lane = lax.broadcasted_iota(jnp.int32, (1, sequence), 1)
    step = 1
    while step < sequence:
        cumulative = cumulative + jnp.where(lane >= step, pltpu.roll(cumulative, step, 1), 0.0)
        step *= 2
    source = jnp.broadcast_to(input_gate - cumulative, (8, sequence)).T[:, 0:1]
    to_t = lax.broadcasted_iota(jnp.int32, (sequence, sequence), 1)
    from_s = lax.broadcasted_iota(jnp.int32, (sequence, sequence), 0)
    out[...] = jnp.exp(jnp.where(from_s <= to_t, cumulative + source, -jnp.inf))


def decay_matrix(own, got, input_bias, forget_bias):
    sequence = own.shape[1]
    return pl.pallas_call(
        decay_kernel,
        in_specs=[VMEM, VMEM, SMEM, SMEM],
        out_specs=VMEM,
        out_shape=jax.ShapeDtypeStruct((sequence, sequence), jnp.float32),
        compiler_params=ROOM,
        name="decay",
    )(own, got, input_bias, forget_bias)


def head_kernel(columns, offsets, *refs):
    count = len(offsets)
    own, got = refs[:count], refs[count : 2 * count]
    last, last_other, tokens, decay, out, projected = refs[2 * count :]
    z, y, x, c = place()
    width, depth = last.shape
    for mine, theirs, offset in zip(own, got, offsets):
        at = pl.multiple_of(lax.bitwise_xor(z, offset) * columns, 16)
        projected[pl.ds(at, columns)] = mine[:columns] + theirs[:columns]
    rest = lax.dot_general(
        last[...], tokens[:, row_block(1 - x, c, depth)], NT, preferred_element_type=jnp.float32
    ) + lax.dot_general(
        last_other[...], tokens[:, row_block(1 - x, 1 - c, depth)], NT, preferred_element_type=jnp.float32
    )
    at = pl.multiple_of(lax.bitwise_xor(z, offsets[-1]) * columns + (1 - y) * width, 16)
    projected[pl.ds(at, width)] += rest
    query, key, value = (projected[n * QK : (n + 1) * QK].astype(jnp.bfloat16) for n in range(3))
    scores = lax.dot_general(key, query, TN, preferred_element_type=jnp.float32) * QK ** (-0.5)
    weighted = scores * decay[...]
    normalizer = jnp.sum(weighted, axis=0, keepdims=True)
    numerator = jnp.dot(value, weighted.astype(jnp.bfloat16), preferred_element_type=jnp.float32)
    out[...] = (numerator / jnp.maximum(jnp.abs(normalizer), 1.0)).T.astype(jnp.bfloat16)


def head(offsets, own, got, last, last_other, tokens, decay):
    sequence = tokens.shape[0]
    columns = NY * last.shape[0]
    return pl.pallas_call(
        functools.partial(head_kernel, columns, offsets),
        in_specs=[VMEM] * (2 * len(offsets) + 4),
        out_specs=VMEM,
        out_shape=jax.ShapeDtypeStruct((sequence, NZ * columns - 2 * QK), jnp.bfloat16),
        scratch_shapes=[pltpu.VMEM((NZ * columns, sequence), jnp.float32)],
        compiler_params=ROOM,
        name="head",
    )(*own, *got, last, last_other, tokens, decay)


def after(value, *others):
    return lax.optimization_barrier((value,) + others)[0]


def by_links(
    tokens, master_weight, first_moment, second_moment, gradient, gate_weight, input_bias, forget_bias
):
    new_master, new_first, new_second, block, gated = adam_step(
        master_weight.T, first_moment.T, second_moment.T, gradient.T, gate_weight.T
    )
    columns = block.shape[0]
    tokens_other = send(tokens, OTHER_CORE)
    z1 = send(block, FLIP_Z[1])
    a1 = send(gated, FIRST)
    a2 = send(gated, SECOND)
    z2 = send(block, FLIP_Z[2])
    held, held_gated = hold(after(tokens, a1), gated)
    b1 = send(z1, FIRST)
    a3 = send(after(a1, z1, held), SECOND)
    b2 = send(after(z1, a2, z2), SECOND)
    z3 = send(after(block, a2), FLIP_Z[3])
    d1 = send(after(z2, b1), FIRST)
    b3 = send(after(b1, b2), SECOND)
    d2 = send(after(z2, a3), SECOND)
    own_a, part_a = project(columns, (held_gated, a1, a2, a3), held, tokens_other)
    got_a = send(part_a, OTHER_CORE)
    d3 = send(d1, SECOND)
    c1 = send(after(z3, own_a), FIRST)
    c2 = send(after(z3, own_a), SECOND)
    own_b, part_b = project(columns, (z1, b1, b2, b3), held, tokens_other)
    got_b = send(part_b, OTHER_CORE)
    decay = decay_matrix(own_a, got_a, input_bias, forget_bias)
    c3 = send(after(c1, own_b, decay), SECOND)
    own_d, part_d = project(columns, (z2, d1, d2, d3), held, tokens_other)
    got_d = send(part_d, OTHER_CORE)
    own_c, part_c = project(columns, (z3, c1, c2), held, tokens_other)
    got_c = send(part_c, OTHER_CORE)
    c3_other = send(c3, OTHER_CORE)
    hidden = head(
        (0, 1, 2, 3), (own_a, own_b, own_d, own_c), (got_a, got_b, got_d, got_c), c3, c3_other, held, decay
    )
    return (new_master.T, new_first.T, new_second.T, hidden)


def solution(mesh):
    placed = (
        P(("group", "inner"), None),
        P("inner", "group"),
        P("inner", "group"),
        P("inner", "group"),
        P("inner", "group"),
        P("inner", None),
        P(),
        P(),
    )
    fits = mesh.shape["group"] == NZ * NY and mesh.shape["inner"] == NX * NC
    return jax.shard_map(
        by_links if fits else gathered_everywhere,
        mesh=mesh,
        in_specs=placed,
        out_specs=(
            P("inner", "group"),
            P("inner", "group"),
            P("inner", "group"),
            P(("group", "inner"), None),
        ),
        check_vma=False,
    )
```

```python
import functools
import itertools

import jax
import jax.numpy as jnp
from jax import lax
from jax.experimental import pallas as pl
from jax.experimental.pallas import tpu as pltpu
from jax.sharding import PartitionSpec as P

QK = 256


beta_first = 0.9
beta_second = 0.999
learn_rate = 0.001
adam_eps = 1e-08
fix_first = 1.0 - (0.9**10) ** 10
fix_second = 1.0 - (0.999**10) ** 10

AXES = ("group", "inner")
NT = (((1,), (1,)), ((), ()))
TN = (((0,), (0,)), ((), ()))


def adam(first_moment, second_moment, master_weight, gradient):
    new_first = beta_first * first_moment + (1.0 - beta_first) * gradient
    new_second = beta_second * second_moment + (1.0 - beta_second) * gradient * gradient
    new_master = master_weight - learn_rate * (new_first / fix_first) / (
        jnp.sqrt(new_second / fix_second) + adam_eps
    )
    return new_master, new_first, new_second


def mlstm_head(sequence, projected, gate_pre, input_bias, forget_bias):
    query_rows = projected[:, :QK].astype(jnp.bfloat16)
    key_rows = projected[:, QK : 2 * QK].astype(jnp.bfloat16)
    value_rows = projected[:, 2 * QK :].astype(jnp.bfloat16)
    input_gate = gate_pre[:, 0] + input_bias[0]
    forget_log = jax.nn.log_sigmoid(gate_pre[:, 1] + forget_bias[0])
    cumulative = jnp.cumsum(forget_log)
    row_count = sequence.shape[0]
    causal = jnp.arange(row_count)[:, None] >= jnp.arange(row_count)[None, :]
    decay_log = cumulative[:, None] - cumulative[None, :] + input_gate[None, :]
    decay_matrix = jnp.exp(jnp.where(causal, decay_log, -jnp.inf))
    scores = jnp.dot(query_rows, key_rows.T, preferred_element_type=jnp.float32) * QK ** (-0.5)
    weighted = scores * decay_matrix
    normalizer = jnp.sum(weighted, axis=1)
    numerator = jnp.dot(
        weighted.astype(jnp.bfloat16), value_rows, preferred_element_type=jnp.float32
    )
    return (numerator / jnp.maximum(jnp.abs(normalizer), 1.0)[:, None]).astype(jnp.bfloat16)


def gathered_everywhere(
    tokens, master_weight, first_moment, second_moment, gradient, gate_weight, input_bias, forget_bias
):
    new_master, new_first, new_second = adam(first_moment, second_moment, master_weight, gradient)
    sendable = new_master.astype(jnp.bfloat16)
    secondary = lax.all_gather(sendable, "group", axis=1, tiled=True)
    projected = jnp.dot(
        tokens,
        lax.all_gather(secondary, "inner", axis=0, tiled=True),
        preferred_element_type=jnp.float32,
    )
    gate_pre = jnp.dot(
        tokens,
        lax.all_gather(gate_weight, "inner", axis=0, tiled=True),
        preferred_element_type=jnp.float32,
    )
    hidden = mlstm_head(tokens, projected, gate_pre, input_bias, forget_bias)
    return (new_master, new_first, new_second, hidden)


NZ, NY, NX, NC = 4, 2, 2, 2


def permutation(target):
    pairs = []
    for z, y, x, c in itertools.product(range(NZ), range(NY), range(NX), range(NC)):
        to_z, to_y, to_x, to_c = target(z, y, x, c)
        pairs.append((((z * NY + y) * NX + x) * NC + c, ((to_z * NY + to_y) * NX + to_x) * NC + to_c))
    return pairs


OTHER_CORE = permutation(lambda z, y, x, c: (z, y, x, 1 - c))
OTHER_X = permutation(lambda z, y, x, c: (z, y, 1 - x, c))
NEXT_Z = permutation(lambda z, y, x, c: ((z + 1) % NZ, y, x, c))
LAST_Z = permutation(lambda z, y, x, c: ((z - 1) % NZ, y, x, c))
FIRST = permutation(lambda z, y, x, c: (z, y, 1 - x, c) if c == 0 else (z, 1 - y, x, c))
SECOND = permutation(lambda z, y, x, c: (z, 1 - y, x, c) if c == 0 else (z, y, 1 - x, c))


def send(block, pairs):
    return lax.ppermute(block, AXES, pairs)


def place():
    group, inner = lax.axis_index("group"), lax.axis_index("inner")
    return group // NY, group % NY, inner // NC, inner % NC


GATE_ROWS = 16


def adam_kernel(
    master_ref, first_ref, second_ref, grad_ref, gate_ref, to_master, to_first, to_second, to_send, to_send_gated
):
    new_master, new_first, new_second = adam(
        first_ref[...], second_ref[...], master_ref[...], grad_ref[...]
    )
    to_master[...] = new_master
    to_first[...] = new_first
    to_second[...] = new_second
    rows = new_master.shape[0]
    at = pl.ds(pl.multiple_of(pl.program_id(0) * rows, 16), rows)
    to_send[at] = new_master.astype(jnp.bfloat16)
    to_send_gated[at] = new_master.astype(jnp.bfloat16)

    @pl.when(pl.program_id(0) == 0)
    def _():
        gate = gate_ref[...]
        pad = jnp.zeros((GATE_ROWS - gate.shape[0], gate.shape[1]), gate.dtype)
        to_send_gated[to_send.shape[0] :] = jnp.concatenate([gate, pad], axis=0)


def adam_step(master, first, second, grad, gate):
    columns, rows = master.shape
    steps = 2
    spec = pl.BlockSpec((columns // steps, rows), lambda i: (i, 0))
    wide = jax.ShapeDtypeStruct(master.shape, jnp.float32)
    sent = [(columns, rows), (columns + GATE_ROWS, rows)]
    return pl.pallas_call(
        adam_kernel,
        grid=(steps,),
        in_specs=[spec] * 4 + [pl.BlockSpec(gate.shape, lambda i: (0, 0))],
        out_specs=[spec] * 3 + [pl.BlockSpec(shape, lambda i: (0, 0)) for shape in sent],
        out_shape=[wide] * 3 + [jax.ShapeDtypeStruct(shape, jnp.bfloat16) for shape in sent],
        name="adam",
    )(master, first, second, grad, gate)


VMEM = pl.BlockSpec(memory_space=pltpu.VMEM)
HBM = pl.BlockSpec(memory_space=pltpu.HBM)
ROOM = pltpu.CompilerParams(vmem_limit_bytes=20 * 2**20)
LONG = pl.CostEstimate(flops=0, bytes_accessed=30 * 2**20, transcendentals=0)
FREE = pl.CostEstimate(flops=0, bytes_accessed=0, transcendentals=0)

def hold_kernel(tokens, gated, input_bias, forget_bias, held, held_gated, biases, sems):
    copies = [
        pltpu.make_async_copy(source, target, sems.at[n])
        for n, (source, target) in enumerate(((tokens, held), (gated, held_gated)))
    ]
    for copy in copies:
        copy.start()
    for n, bias in enumerate((input_bias, forget_bias)):
        biases[n] = jnp.broadcast_to(bias[...], biases.shape[1:])
    for copy in copies:
        copy.wait()


def hold(tokens, gated, input_bias, forget_bias):
    return pl.pallas_call(
        hold_kernel,
        in_specs=[HBM] * 2 + [VMEM] * 2,
        out_specs=[VMEM] * 3,
        out_shape=[jax.ShapeDtypeStruct(array.shape, array.dtype) for array in (tokens, gated)]
        + [jax.ShapeDtypeStruct((2, 8, tokens.shape[0]), jnp.float32)],
        scratch_shapes=[pltpu.SemaphoreType.DMA((2,))],
        compiler_params=ROOM,
        cost_estimate=LONG,
        name="hold",
    )(tokens, gated, input_bias.reshape(1, 1), forget_bias.reshape(1, 1))


def row_block(its_x, its_c, depth):
    return pl.ds(pl.multiple_of((its_x * NC + its_c) * depth, depth), depth)


def project_kernel(columns, gathers, gated, *refs):
    *blocks, tokens, tokens_other, out_own, out_send, stack = refs
    _, y, x, c = place()
    depth = blocks[0].shape[1]
    swap = c == 0
    spots = (
        (0, y),
        (jnp.where(swap, 1, 0), jnp.where(swap, y, 1 - y)),
        (jnp.where(swap, 0, 1), jnp.where(swap, 1 - y, y)),
        (1, 1 - y),
    )
    gathered = [blocks[sum(gathers[:n]) :][:count] for n, count in enumerate(gathers)]
    for n, its_blocks in enumerate(gathered):
        for k, (side, its_y) in enumerate(spots):
            at = pl.ds(pl.multiple_of((n * NY + its_y) * columns, 16), columns)
            if k < len(its_blocks):
                stack[side, at] = its_blocks[k][:columns]
            else:
                stack[side, at] = jnp.zeros((columns, depth), jnp.bfloat16)
    if gated is not None:
        own, first, second = (block[columns:] for block in gathered[gated][:3])
        stack[0, len(gathers) * NY * columns :] = own
        stack[1, len(gathers) * NY * columns :] = jnp.where(swap, first, second)
    for source, out in ((tokens_other, out_send), (tokens, out_own)):
        parts = [
            lax.dot_general(
                stack[side], source[:, row_block(its_x, c, depth)], NT, preferred_element_type=jnp.float32
            )
            for side, its_x in enumerate((x, 1 - x))
        ]
        out[...] = parts[0] + parts[1]


def project(columns, gathered, tokens, tokens_other, gated=None):
    blocks = [block for its_blocks in gathered for block in its_blocks]
    depth = blocks[0].shape[1]
    rows = len(gathered) * NY * columns + (0 if gated is None else GATE_ROWS)
    sequence = tokens.shape[0]
    out = jax.ShapeDtypeStruct((rows, sequence), jnp.float32)
    return pl.pallas_call(
        functools.partial(project_kernel, columns, [len(its_blocks) for its_blocks in gathered], gated),
        in_specs=[VMEM] * (len(blocks) + 2),
        out_specs=[VMEM] * 2,
        out_shape=[out, out],
        scratch_shapes=[pltpu.VMEM((NX, rows, depth), jnp.bfloat16)],
        compiler_params=ROOM,
        cost_estimate=FREE,
        name="project",
    )(*blocks, tokens, tokens_other)


def decay_kernel(own, got, biases, out):
    rows, sequence = own.shape
    gate_pre = own[rows - GATE_ROWS : rows - 8] + got[rows - GATE_ROWS : rows - 8]
    input_gate = gate_pre[0:1] + biases[0, 0:1]
    cumulative = jax.nn.log_sigmoid(gate_pre[1:2] + biases[1, 0:1])
    lane = lax.broadcasted_iota(jnp.int32, (1, sequence), 1)
    step = 1
    while step < sequence:
        cumulative = cumulative + jnp.where(lane >= step, pltpu.roll(cumulative, step, 1), 0.0)
        step *= 2
    by_row = jnp.concatenate([cumulative, input_gate, jnp.zeros((6, sequence), jnp.float32)], axis=0).T
    to_t = lax.broadcasted_iota(jnp.int32, (sequence, sequence), 1)
    from_s = lax.broadcasted_iota(jnp.int32, (sequence, sequence), 0)
    out[...] = jnp.exp(jnp.where(from_s <= to_t, cumulative - by_row[:, 0:1] + by_row[:, 1:2], -jnp.inf))


def decay_matrix(own, got, biases):
    sequence = own.shape[1]
    return pl.pallas_call(
        decay_kernel,
        in_specs=[VMEM] * 3,
        out_specs=VMEM,
        out_shape=jax.ShapeDtypeStruct((sequence, sequence), jnp.float32),
        compiler_params=ROOM,
        name="decay",
    )(own, got, biases)


def pending_rows(offset, width):
    z, y, _, _ = place()
    return pl.ds(pl.multiple_of((lax.rem(z + offset, NZ) * NY + 1 - y) * width, 16), width)


def assemble_kernel(columns, offsets, *refs):
    own, got = refs[: len(offsets)], refs[len(offsets) : 2 * len(offsets)]
    last, tokens, projected, pending = refs[2 * len(offsets) :]
    z, _, x, c = place()
    width, depth = last.shape
    at = row_block(1 - x, c, depth)
    rest = lax.dot_general(last[...], tokens[:, at], NT, preferred_element_type=jnp.float32)
    for mine, theirs, its_offsets in zip(own, got, offsets):
        for n, offset in enumerate(its_offsets):
            at = pl.multiple_of(lax.rem(z + offset, NZ) * columns, 16)
            rows = slice(n * columns, (n + 1) * columns)
            projected[pl.ds(at, columns)] = (mine[rows] + theirs[rows]).astype(jnp.bfloat16)
    _, y, _, _ = place()
    rows = pl.ds(pl.multiple_of((len(offsets[-1]) - 1) * columns + (1 - y) * width, 16), width)
    pending[...] = own[-1][rows] + got[-1][rows] + rest


def assemble(offsets, own, got, last, tokens):
    sequence = tokens.shape[0]
    width = last.shape[0]
    return pl.pallas_call(
        functools.partial(assemble_kernel, NY * width, offsets),
        in_specs=[VMEM] * (2 * len(offsets) + 2),
        out_specs=[VMEM] * 2,
        out_shape=[
            jax.ShapeDtypeStruct((NZ * NY * width, sequence), jnp.bfloat16),
            jax.ShapeDtypeStruct((width, sequence), jnp.float32),
        ],
        compiler_params=ROOM,
        name="assemble",
    )(*own, *got, last, tokens)


def head_kernel(offset, assembled, pending, last_other, tokens, decay, out, projected):
    _, _, x, c = place()
    width, depth = last_other.shape
    at = row_block(1 - x, 1 - c, depth)
    rest = lax.dot_general(last_other[...], tokens[:, at], NT, preferred_element_type=jnp.float32)
    projected[...] = assembled[...]
    projected[pending_rows(offset, width)] = (pending[...] + rest).astype(jnp.bfloat16)
    query, key, value = (projected[n * QK : (n + 1) * QK] for n in range(3))
    scores = lax.dot_general(key, query, TN, preferred_element_type=jnp.float32) * QK ** (-0.5)
    weighted = scores * decay[...]
    normalizer = jnp.sum(weighted, axis=0, keepdims=True)
    numerator = jnp.dot(value, weighted.astype(jnp.bfloat16), preferred_element_type=jnp.float32)
    out[...] = (numerator / jnp.maximum(jnp.abs(normalizer), 1.0)).T.astype(jnp.bfloat16)


def head(offset, assembled, pending, last_other, tokens, decay):
    columns, sequence = assembled.shape
    return pl.pallas_call(
        functools.partial(head_kernel, offset),
        in_specs=[VMEM] * 5,
        out_specs=VMEM,
        out_shape=jax.ShapeDtypeStruct((sequence, columns - 2 * QK), jnp.bfloat16),
        scratch_shapes=[pltpu.VMEM(assembled.shape, jnp.bfloat16)],
        compiler_params=ROOM,
        name="head",
    )(assembled, pending, last_other, tokens, decay)


def after(value, *others):
    return lax.optimization_barrier((value,) + others)[0]


def by_links(
    tokens, master_weight, first_moment, second_moment, gradient, gate_weight, input_bias, forget_bias
):
    new_master, new_first, new_second, block, gated = adam_step(
        master_weight.T, first_moment.T, second_moment.T, gradient.T, gate_weight.T
    )
    columns = block.shape[0]
    tokens_other = send(tokens, OTHER_CORE)
    z1 = send(gated, NEXT_Z)
    a1 = send(block, FIRST)
    a2 = send(block, SECOND)
    z2 = send(block, LAST_Z)
    held, held_block, biases = hold(tokens, block, input_bias, forget_bias)
    a3 = send(after(a1, held), SECOND)
    b1 = send(after(z1, held), FIRST)
    b2 = send(after(z1, a2, z2), SECOND)
    z3 = send(z2, LAST_Z)
    d1 = send(after(z2, b1, a3), FIRST)
    b3 = send(after(b1, b2), SECOND)
    d2 = send(after(z2, a3, z3, b2), SECOND)
    own_a, part_a = project(columns, ((held_block, a1, a2, a3),), held, tokens_other)
    d3 = send(d1, SECOND)
    c1 = send(after(z3, own_a), FIRST)
    got_a = send(after(part_a, c1), OTHER_CORE)
    c2 = send(after(z3, b3), SECOND)
    own_b, part_b = project(columns, ((z1, b1, b2, b3),), held, tokens_other, 0)
    got_b = send(part_b, OTHER_CORE)
    c3 = send(after(c1, own_b), SECOND)
    decay = decay_matrix(own_b, got_b, biases)
    own_d, part_d = project(columns, ((z2, d1, d2, d3),), held, tokens_other)
    got_d = send(part_d, OTHER_CORE)
    own_c, part_c = project(columns, ((z3, c1, c2),), held, tokens_other)
    got_c = send(part_c, OTHER_CORE)
    c3_other = send(c3, OTHER_CORE)
    assembled, pending = assemble(
        ((0,), (3,), (1,), (2,)), (own_a, own_b, own_d, own_c), (got_a, got_b, got_d, got_c), c3, held
    )
    hidden = head(2, assembled, pending, c3_other, held, decay)
    return (new_master.T, new_first.T, new_second.T, hidden)


def solution(mesh):
    placed = (
        P(("group", "inner"), None),
        P("inner", "group"),
        P("inner", "group"),
        P("inner", "group"),
        P("inner", "group"),
        P("inner", None),
        P(),
        P(),
    )
    fits = mesh.shape["group"] == NZ * NY and mesh.shape["inner"] == NX * NC
    return jax.shard_map(
        by_links if fits else gathered_everywhere,
        mesh=mesh,
        in_specs=placed,
        out_specs=(
            P("inner", "group"),
            P("inner", "group"),
            P("inner", "group"),
            P(("group", "inner"), None),
        ),
        check_vma=False,
    )
```

```python
import functools
import itertools

import jax
import jax.numpy as jnp
from jax import lax
from jax.experimental import pallas as pl
from jax.experimental.pallas import tpu as pltpu
from jax.sharding import PartitionSpec as P

QK = 256


beta_first = 0.9
beta_second = 0.999
learn_rate = 0.001
adam_eps = 1e-08
fix_first = 1.0 - (0.9**10) ** 10
fix_second = 1.0 - (0.999**10) ** 10

AXES = ("group", "inner")
NT = (((1,), (1,)), ((), ()))
TN = (((0,), (0,)), ((), ()))


def adam(first_moment, second_moment, master_weight, gradient):
    new_first = beta_first * first_moment + (1.0 - beta_first) * gradient
    new_second = beta_second * second_moment + (1.0 - beta_second) * gradient * gradient
    new_master = master_weight - learn_rate * (new_first / fix_first) / (
        jnp.sqrt(new_second / fix_second) + adam_eps
    )
    return new_master, new_first, new_second


def mlstm_head(sequence, projected, gate_pre, input_bias, forget_bias):
    query_rows = projected[:, :QK].astype(jnp.bfloat16)
    key_rows = projected[:, QK : 2 * QK].astype(jnp.bfloat16)
    value_rows = projected[:, 2 * QK :].astype(jnp.bfloat16)
    input_gate = gate_pre[:, 0] + input_bias[0]
    forget_log = jax.nn.log_sigmoid(gate_pre[:, 1] + forget_bias[0])
    cumulative = jnp.cumsum(forget_log)
    row_count = sequence.shape[0]
    causal = jnp.arange(row_count)[:, None] >= jnp.arange(row_count)[None, :]
    decay_log = cumulative[:, None] - cumulative[None, :] + input_gate[None, :]
    decay_matrix = jnp.exp(jnp.where(causal, decay_log, -jnp.inf))
    scores = jnp.dot(query_rows, key_rows.T, preferred_element_type=jnp.float32) * QK ** (-0.5)
    weighted = scores * decay_matrix
    normalizer = jnp.sum(weighted, axis=1)
    numerator = jnp.dot(
        weighted.astype(jnp.bfloat16), value_rows, preferred_element_type=jnp.float32
    )
    return (numerator / jnp.maximum(jnp.abs(normalizer), 1.0)[:, None]).astype(jnp.bfloat16)


def gathered_everywhere(
    tokens, master_weight, first_moment, second_moment, gradient, gate_weight, input_bias, forget_bias
):
    new_master, new_first, new_second = adam(first_moment, second_moment, master_weight, gradient)
    sendable = new_master.astype(jnp.bfloat16)
    secondary = lax.all_gather(sendable, "group", axis=1, tiled=True)
    projected = jnp.dot(
        tokens,
        lax.all_gather(secondary, "inner", axis=0, tiled=True),
        preferred_element_type=jnp.float32,
    )
    gate_pre = jnp.dot(
        tokens,
        lax.all_gather(gate_weight, "inner", axis=0, tiled=True),
        preferred_element_type=jnp.float32,
    )
    hidden = mlstm_head(tokens, projected, gate_pre, input_bias, forget_bias)
    return (new_master, new_first, new_second, hidden)


NZ, NY, NX, NC = 4, 2, 2, 2


def permutation(target):
    pairs = []
    for z, y, x, c in itertools.product(range(NZ), range(NY), range(NX), range(NC)):
        to_z, to_y, to_x, to_c = target(z, y, x, c)
        pairs.append((((z * NY + y) * NX + x) * NC + c, ((to_z * NY + to_y) * NX + to_x) * NC + to_c))
    return pairs


OTHER_CORE = permutation(lambda z, y, x, c: (z, y, x, 1 - c))
OTHER_X = permutation(lambda z, y, x, c: (z, y, 1 - x, c))
NEXT_Z = permutation(lambda z, y, x, c: ((z + 1) % NZ, y, x, c))
LAST_Z = permutation(lambda z, y, x, c: ((z - 1) % NZ, y, x, c))
FIRST = permutation(lambda z, y, x, c: (z, y, 1 - x, c) if c == 0 else (z, 1 - y, x, c))
SECOND = permutation(lambda z, y, x, c: (z, 1 - y, x, c) if c == 0 else (z, y, 1 - x, c))


def send(block, pairs):
    return lax.ppermute(block, AXES, pairs)


def place():
    group, inner = lax.axis_index("group"), lax.axis_index("inner")
    return group // NY, group % NY, inner // NC, inner % NC


GATE_ROWS = 16


def adam_kernel(
    master_ref, first_ref, second_ref, grad_ref, gate_ref, to_master, to_first, to_second, to_send, to_send_gated
):
    new_master, new_first, new_second = adam(
        first_ref[...], second_ref[...], master_ref[...], grad_ref[...]
    )
    to_master[...] = new_master
    to_first[...] = new_first
    to_second[...] = new_second
    rows = new_master.shape[0]
    at = pl.ds(pl.multiple_of(pl.program_id(0) * rows, 16), rows)
    to_send[at] = new_master.astype(jnp.bfloat16)
    to_send_gated[at] = new_master.astype(jnp.bfloat16)

    @pl.when(pl.program_id(0) == 0)
    def _():
        gate = gate_ref[...]
        pad = jnp.zeros((GATE_ROWS - gate.shape[0], gate.shape[1]), gate.dtype)
        to_send_gated[to_send.shape[0] :] = jnp.concatenate([gate, pad], axis=0)


def adam_step(master, first, second, grad, gate):
    columns, rows = master.shape
    steps = 2
    spec = pl.BlockSpec((columns // steps, rows), lambda i: (i, 0))
    wide = jax.ShapeDtypeStruct(master.shape, jnp.float32)
    sent = [(columns, rows), (columns + GATE_ROWS, rows)]
    return pl.pallas_call(
        adam_kernel,
        grid=(steps,),
        in_specs=[spec] * 4 + [pl.BlockSpec(gate.shape, lambda i: (0, 0))],
        out_specs=[spec] * 3 + [pl.BlockSpec(shape, lambda i: (0, 0)) for shape in sent],
        out_shape=[wide] * 3 + [jax.ShapeDtypeStruct(shape, jnp.bfloat16) for shape in sent],
        name="adam",
    )(master, first, second, grad, gate)


VMEM = pl.BlockSpec(memory_space=pltpu.VMEM)
HBM = pl.BlockSpec(memory_space=pltpu.HBM)
ROOM = pltpu.CompilerParams(vmem_limit_bytes=20 * 2**20)
LONG = pl.CostEstimate(flops=0, bytes_accessed=30 * 2**20, transcendentals=0)
FREE = pl.CostEstimate(flops=0, bytes_accessed=0, transcendentals=0)

def hold_kernel(tokens, gated, input_bias, forget_bias, held, held_gated, biases, sems):
    copies = [
        pltpu.make_async_copy(source, target, sems.at[n])
        for n, (source, target) in enumerate(((tokens, held), (gated, held_gated)))
    ]
    for copy in copies:
        copy.start()
    for n, bias in enumerate((input_bias, forget_bias)):
        biases[n] = jnp.broadcast_to(bias[...], biases.shape[1:])
    for copy in copies:
        copy.wait()


def hold(tokens, gated, input_bias, forget_bias):
    return pl.pallas_call(
        hold_kernel,
        in_specs=[HBM] * 2 + [VMEM] * 2,
        out_specs=[VMEM] * 3,
        out_shape=[jax.ShapeDtypeStruct(array.shape, array.dtype) for array in (tokens, gated)]
        + [jax.ShapeDtypeStruct((2, 8, tokens.shape[0]), jnp.float32)],
        scratch_shapes=[pltpu.SemaphoreType.DMA((2,))],
        compiler_params=ROOM,
        cost_estimate=LONG,
        name="hold",
    )(tokens, gated, input_bias.reshape(1, 1), forget_bias.reshape(1, 1))


def row_block(its_x, its_c, depth):
    return pl.ds(pl.multiple_of((its_x * NC + its_c) * depth, depth), depth)


def project_kernel(columns, gathers, gated, *refs):
    *blocks, tokens, tokens_other, out_own, out_send, stack = refs
    _, y, x, c = place()
    depth = blocks[0].shape[1]
    swap = c == 0
    spots = (
        (0, y),
        (jnp.where(swap, 1, 0), jnp.where(swap, y, 1 - y)),
        (jnp.where(swap, 0, 1), jnp.where(swap, 1 - y, y)),
        (1, 1 - y),
    )
    gathered = [blocks[sum(gathers[:n]) :][:count] for n, count in enumerate(gathers)]
    for n, its_blocks in enumerate(gathered):
        for k, (side, its_y) in enumerate(spots):
            at = pl.ds(pl.multiple_of((n * NY + its_y) * columns, 16), columns)
            if k < len(its_blocks):
                stack[side, at] = its_blocks[k][:columns]
            else:
                stack[side, at] = jnp.zeros((columns, depth), jnp.bfloat16)
    if gated is not None:
        own, first, second = (block[columns:] for block in gathered[gated][:3])
        stack[0, len(gathers) * NY * columns :] = own
        stack[1, len(gathers) * NY * columns :] = jnp.where(swap, first, second)
    for source, out in ((tokens_other, out_send), (tokens, out_own)):
        parts = [
            lax.dot_general(
                stack[side], source[:, row_block(its_x, c, depth)], NT, preferred_element_type=jnp.float32
            )
            for side, its_x in enumerate((x, 1 - x))
        ]
        out[...] = parts[0] + parts[1]


def project(columns, gathered, tokens, tokens_other, gated=None):
    blocks = [block for its_blocks in gathered for block in its_blocks]
    depth = blocks[0].shape[1]
    rows = len(gathered) * NY * columns + (0 if gated is None else GATE_ROWS)
    sequence = tokens.shape[0]
    out = jax.ShapeDtypeStruct((rows, sequence), jnp.float32)
    return pl.pallas_call(
        functools.partial(project_kernel, columns, [len(its_blocks) for its_blocks in gathered], gated),
        in_specs=[VMEM] * (len(blocks) + 2),
        out_specs=[VMEM] * 2,
        out_shape=[out, out],
        scratch_shapes=[pltpu.VMEM((NX, rows, depth), jnp.bfloat16)],
        compiler_params=ROOM,
        cost_estimate=FREE,
        name="project",
    )(*blocks, tokens, tokens_other)


def decay_kernel(own, got, biases, out):
    rows, sequence = own.shape
    gate_pre = own[rows - GATE_ROWS : rows - 8] + got[rows - GATE_ROWS : rows - 8]
    input_gate = gate_pre[0:1] + biases[0, 0:1]
    cumulative = jax.nn.log_sigmoid(gate_pre[1:2] + biases[1, 0:1])
    lane = lax.broadcasted_iota(jnp.int32, (1, sequence), 1)
    step = 1
    while step < sequence:
        cumulative = cumulative + jnp.where(lane >= step, pltpu.roll(cumulative, step, 1), 0.0)
        step *= 2
    by_row = jnp.concatenate([cumulative, input_gate, jnp.zeros((6, sequence), jnp.float32)], axis=0).T
    to_t = lax.broadcasted_iota(jnp.int32, (sequence, sequence), 1)
    from_s = lax.broadcasted_iota(jnp.int32, (sequence, sequence), 0)
    out[...] = jnp.exp(jnp.where(from_s <= to_t, cumulative - by_row[:, 0:1] + by_row[:, 1:2], -jnp.inf))


def decay_matrix(own, got, biases):
    sequence = own.shape[1]
    return pl.pallas_call(
        decay_kernel,
        in_specs=[VMEM] * 3,
        out_specs=VMEM,
        out_shape=jax.ShapeDtypeStruct((sequence, sequence), jnp.float32),
        compiler_params=ROOM,
        name="decay",
    )(own, got, biases)


def pending_rows(offset, width):
    z, y, _, _ = place()
    return pl.ds(pl.multiple_of((lax.rem(z + offset, NZ) * NY + 1 - y) * width, 16), width)


def assemble_kernel(columns, offsets, *refs):
    own, got = refs[: len(offsets)], refs[len(offsets) : 2 * len(offsets)]
    last, tokens, projected, pending = refs[2 * len(offsets) :]
    z, _, x, c = place()
    width, depth = last.shape
    at = row_block(1 - x, c, depth)
    rest = lax.dot_general(last[...], tokens[:, at], NT, preferred_element_type=jnp.float32)
    for mine, theirs, its_offsets in zip(own, got, offsets):
        for n, offset in enumerate(its_offsets):
            at = pl.multiple_of(lax.rem(z + offset, NZ) * columns, 16)
            rows = slice(n * columns, (n + 1) * columns)
            projected[pl.ds(at, columns)] = (mine[rows] + theirs[rows]).astype(jnp.bfloat16)
    _, y, _, _ = place()
    rows = pl.ds(pl.multiple_of((len(offsets[-1]) - 1) * columns + (1 - y) * width, 16), width)
    pending[...] = own[-1][rows] + got[-1][rows] + rest


def assemble(offsets, own, got, last, tokens):
    sequence = tokens.shape[0]
    width = last.shape[0]
    return pl.pallas_call(
        functools.partial(assemble_kernel, NY * width, offsets),
        in_specs=[VMEM] * (2 * len(offsets) + 2),
        out_specs=[VMEM] * 2,
        out_shape=[
            jax.ShapeDtypeStruct((NZ * NY * width, sequence), jnp.bfloat16),
            jax.ShapeDtypeStruct((width, sequence), jnp.float32),
        ],
        compiler_params=ROOM,
        name="assemble",
    )(*own, *got, last, tokens)


def head_kernel(offset, assembled, pending, last_other, tokens, decay, out, projected):
    _, _, x, c = place()
    width, depth = last_other.shape
    at = row_block(1 - x, 1 - c, depth)
    rest = lax.dot_general(last_other[...], tokens[:, at], NT, preferred_element_type=jnp.float32)
    projected[...] = assembled[...]
    projected[pending_rows(offset, width)] = (pending[...] + rest).astype(jnp.bfloat16)
    query, key, value = (projected[n * QK : (n + 1) * QK] for n in range(3))
    scores = lax.dot_general(key, query, TN, preferred_element_type=jnp.float32) * QK ** (-0.5)
    weighted = scores * decay[...]
    normalizer = jnp.sum(weighted, axis=0, keepdims=True)
    numerator = jnp.dot(value, weighted.astype(jnp.bfloat16), preferred_element_type=jnp.float32)
    out[...] = (numerator / jnp.maximum(jnp.abs(normalizer), 1.0)).astype(jnp.bfloat16).T


def head(offset, assembled, pending, last_other, tokens, decay):
    columns, sequence = assembled.shape
    return pl.pallas_call(
        functools.partial(head_kernel, offset),
        in_specs=[VMEM] * 5,
        out_specs=VMEM,
        out_shape=jax.ShapeDtypeStruct((sequence, columns - 2 * QK), jnp.bfloat16),
        scratch_shapes=[pltpu.VMEM(assembled.shape, jnp.bfloat16)],
        compiler_params=ROOM,
        name="head",
    )(assembled, pending, last_other, tokens, decay)


def after(value, *others):
    return lax.optimization_barrier((value,) + others)[0]


def by_links(
    tokens, master_weight, first_moment, second_moment, gradient, gate_weight, input_bias, forget_bias
):
    new_master, new_first, new_second, block, gated = adam_step(
        master_weight.T, first_moment.T, second_moment.T, gradient.T, gate_weight.T
    )
    columns = block.shape[0]
    tokens_other = send(tokens, OTHER_CORE)
    z1 = send(gated, NEXT_Z)
    a1 = send(block, FIRST)
    a2 = send(block, SECOND)
    z2 = send(block, LAST_Z)
    held, held_block, biases = hold(tokens, block, input_bias, forget_bias)
    a3 = send(after(a1, held), SECOND)
    b1 = send(after(z1, held), FIRST)
    b2 = send(after(z1, a2, z2), SECOND)
    z3 = send(z2, LAST_Z)
    d1 = send(after(z2, b1, a3), FIRST)
    b3 = send(after(b1, b2), SECOND)
    d2 = send(after(z2, a3, z3, b2), SECOND)
    own_a, part_a = project(columns, ((held_block, a1, a2, a3),), held, tokens_other)
    d3 = send(d1, SECOND)
    c1 = send(after(z3, own_a), FIRST)
    got_a = send(after(part_a, c1), OTHER_CORE)
    c2 = send(after(z3, b3), SECOND)
    own_b, part_b = project(columns, ((z1, b1, b2, b3),), held, tokens_other, 0)
    got_b = send(part_b, OTHER_CORE)
    c3 = send(after(c1, own_b), SECOND)
    decay = decay_matrix(own_b, got_b, biases)
    own_d, part_d = project(columns, ((z2, d1, d2, d3),), held, tokens_other)
    got_d = send(part_d, OTHER_CORE)
    own_c, part_c = project(columns, ((z3, c1, c2),), held, tokens_other)
    got_c = send(part_c, OTHER_CORE)
    c3_other = send(c3, OTHER_CORE)
    assembled, pending = assemble(
        ((0,), (3,), (1,), (2,)), (own_a, own_b, own_d, own_c), (got_a, got_b, got_d, got_c), c3, held
    )
    hidden = head(2, assembled, pending, c3_other, held, decay)
    return (new_master.T, new_first.T, new_second.T, hidden)


def solution(mesh):
    placed = (
        P(("group", "inner"), None),
        P("inner", "group"),
        P("inner", "group"),
        P("inner", "group"),
        P("inner", "group"),
        P("inner", None),
        P(),
        P(),
    )
    fits = mesh.shape["group"] == NZ * NY and mesh.shape["inner"] == NX * NC
    return jax.shard_map(
        by_links if fits else gathered_everywhere,
        mesh=mesh,
        in_specs=placed,
        out_specs=(
            P("inner", "group"),
            P("inner", "group"),
            P("inner", "group"),
            P(("group", "inner"), None),
        ),
        check_vma=False,
    )
```
